32 devices in a mesh: dp: 8 (over z, y), mp: 4 (over x, core).
Axes of the slice: x: 2, y: 2, z: 4, core: 2. Of those that a mesh axis runs over, the one named last changes fastest.
Arguments:
- tokens: bfloat16 [4096, 1152], P(('dp', 'mp')), may hold values from -6 to 6
- segment_ids: int32 [4096], P('dp'), may hold values from 0 to 2, as said below
- positions: int32 [4096], P('dp'), may hold values from 0 to 5118, as said below
- q_weight: bfloat16 [1152, 1024], P('dp', 'mp'), may hold values from -0.1875 to 0.1875
- kv_weight: bfloat16 [1152, 512], P('dp'), may hold values from -0.1875 to 0.1875
- o_weight: bfloat16 [1024, 1152], P('mp', 'dp'), may hold values from -0.1875 to 0.1875
- gate_up_weight: bfloat16 [2, 1152, 6912], P(None, 'dp', 'mp'), may hold values from -0.1875 to 0.1875
- down_weight: bfloat16 [6912, 1152], P('mp', 'dp'), may hold values from -0.078125 to 0.078125
- attn_pre_gain: bfloat16 [1152], P('dp'), may hold values from 0.25 to 1.75
- attn_post_gain: bfloat16 [1152], P('dp'), may hold values from 0.25 to 1.75
- ff_pre_gain: bfloat16 [1152], P('dp'), may hold values from 0.25 to 1.75
- ff_post_gain: bfloat16 [1152], P('dp'), may hold values from 0.25 to 1.75
- query_gain: bfloat16 [256], P('dp'), may hold values from 0.25 to 1.75
- key_gain: bfloat16 [256], P('dp'), may hold values from 0.25 to 1.75
- out_grad: bfloat16 [4096, 1152], P(('dp', 'mp')), may hold values from -6 to 6
Outputs:
- out: bfloat16 [4096, 1152], P(('dp', 'mp'))
- tokens_grad: float32 [4096, 1152], P(('dp', 'mp'))
- q_weight_grad: float32 [1152, 1024], P('dp', 'mp')
- kv_weight_grad: float32 [1152, 512], P('dp')
- o_weight_grad: float32 [1024, 1152], P('mp', 'dp')
- gate_up_weight_grad: float32 [2, 1152, 6912], P(None, 'dp', 'mp')
- down_weight_grad: float32 [6912, 1152], P('mp', 'dp')
- attn_pre_gain_grad: float32 [1152], P('dp')
- attn_post_gain_grad: float32 [1152], P('dp')
- ff_pre_gain_grad: float32 [1152], P('dp')
- ff_post_gain_grad: float32 [1152], P('dp')
- query_gain_grad: float32 [256], P('dp')
- key_gain_grad: float32 [256], P('dp')
The draws below stay inside these ranges and needn't reach their ends.
Inputs may be any that keep to these rules, and one draw needn't show every extreme that they name: `segment_ids`: segment ids never fall; document 0 and document 2 each hold 1 to 256 tokens, document 1 the rest. Within a document, positions rise by one from token to token; document 0 starts at position 0, document 2 at 0 to 1023, and the last token of document 1 has position 5118.
All inputs are finite; a program needn't handle non-finite values.
Results may differ from the reference program's by a relative error of at most 0.028.
Values may be sent and summed in bfloat16 or wider, within the bound.
A program may use at most 128 MiB of HBM per device.

```python
import jax
import jax.numpy as jnp
from jax import lax

D = 1152
HEADS = 4
HD = 256
FF = 6912
WINDOW = 512
TOK_DEV = 512
TOKENS = 4096


def document_bounds(key):
    front_key, back_key = jax.random.split(key)
    front = jax.random.randint(front_key, (), 1, TOK_DEV // 2 + 1)
    back = TOKENS - jax.random.randint(back_key, (), 1, TOK_DEV // 2 + 1)
    index = jnp.arange(TOKENS, dtype=jnp.int32)
    documents = (index >= front).astype(jnp.int32) + (index >= back).astype(jnp.int32)
    return (index, front, back, documents)


def draw_segment_ids(key, part):
    index, front, back, documents = document_bounds(key)
    return documents


def draw_positions(key, part):
    index, front, back, documents = document_bounds(key)
    key = jax.random.fold_in(key, 7)
    opening = jax.random.randint(key, (), 0, 1024)
    middle_start = 1023 + TOKENS - (back - front)
    begin = jnp.where(documents == 0, 0, jnp.where(documents == 1, front, back))
    offset = jnp.where(documents == 0, 0, jnp.where(documents == 1, middle_start, opening))
    return (offset + index - begin).astype(jnp.int32)


def level_of(own_key, dims, cuts, smallest, largest):
    def one(position, parts):
        draws = jax.random.uniform(jax.random.fold_in(jax.random.fold_in(own_key, 6), position), (parts,), jnp.float32, smallest / len(cuts), largest / len(cuts))
        return jnp.repeat(jnp.exp(draws), dims[position] // parts).reshape((-1,) + (1,) * (len(dims) - position - 1))

    level = one(*cuts[0])
    for cut in cuts[1:]:
        level = level * one(*cut)
    return level


def gaussian(key, shape, deviation, reach, shards=(), kind=jnp.bfloat16):
    level = level_of(key, shape, shards, -0.22, 0.18) if shards else 1.0
    values = jax.random.normal(key, shape, jnp.float32) * deviation * level
    return jnp.minimum(jnp.maximum(values, -reach), reach).astype(kind)


def setup_inputs(seed: int = 0) -> dict:
    splits = jax.random.split(jax.random.key(seed), 16)
    return {
        "tokens": gaussian(splits[0], (TOKENS, D), 1.0, 6.0, ((0, 32),)),
        "segment_ids": draw_segment_ids(jax.random.fold_in(splits[15], 71), 0),
        "positions": draw_positions(jax.random.fold_in(splits[15], 71), 0),
        "q_weight": gaussian(splits[3], (D, HEADS * HD), D ** -0.5, 0.1875, ((0, 8), (1, 4))),
        "kv_weight": gaussian(splits[4], (D, 2 * HD), D ** -0.5, 0.1875, ((0, 8),)),
        "o_weight": gaussian(splits[5], (HEADS * HD, D), (HEADS * HD) ** -0.5, 0.1875, ((0, 4), (1, 8))),
        "gate_up_weight": gaussian(splits[6], (2, D, FF), D ** -0.5, 0.1875, ((1, 8), (2, 4))),
        "down_weight": gaussian(splits[7], (FF, D), FF ** -0.5, 0.078125, ((0, 4), (1, 8))),
        "attn_pre_gain": jnp.clip(1.0 + 0.15 * jax.random.normal(splits[8], (D,), jnp.float32), 0.25, 1.75).astype(jnp.bfloat16),
        "attn_post_gain": jnp.clip(1.0 + 0.15 * jax.random.normal(splits[9], (D,), jnp.float32), 0.25, 1.75).astype(jnp.bfloat16),
        "ff_pre_gain": jnp.clip(1.0 + 0.15 * jax.random.normal(splits[10], (D,), jnp.float32), 0.25, 1.75).astype(jnp.bfloat16),
        "ff_post_gain": jnp.clip(1.0 + 0.15 * jax.random.normal(splits[11], (D,), jnp.float32), 0.25, 1.75).astype(jnp.bfloat16),
        "query_gain": jnp.clip(1.0 + 0.15 * jax.random.normal(splits[12], (HD,), jnp.float32), 0.25, 1.75).astype(jnp.bfloat16),
        "key_gain": jnp.clip(1.0 + 0.15 * jax.random.normal(splits[13], (HD,), jnp.float32), 0.25, 1.75).astype(jnp.bfloat16),
        "out_grad": gaussian(splits[14], (TOKENS, D), 1.0, 6.0, ((0, 32),)),
    }


EPS = 1e-06
NEG = -1e+30
HIGH = lax.Precision.HIGHEST

@jax.custom_vjp
def low(v):
    return lax.optimization_barrier(v.astype(jnp.bfloat16)).astype(jnp.float32)

@jax.custom_vjp
def low_back(v):
    return v

def low_keep(v):
    return (low(v), None)

def low_pass(kept, grad):
    return (grad,)

def back_keep(v):
    return (v, None)

def back_low(kept, grad):
    return (low(grad),)
low.defvjp(low_keep, low_pass)
low_back.defvjp(back_keep, back_low)

def normalize(value, gain):
    return value * lax.rsqrt(lax.optimization_barrier(jnp.mean(value * value, axis=-1, keepdims=True)) + EPS) * gain

def rotary_tables(positions, width):
    half_width = width // 2
    frequency = jnp.power(10000.0, -jnp.arange(half_width, dtype=jnp.float32) * (2.0 / width))
    angles = positions.astype(jnp.float32)[:, None] * frequency[None, :]
    return (jnp.cos(angles), jnp.sin(angles))

def rotate(value, cosine, sine):
    half_width = value.shape[-1] // 2
    first_half = value[..., :half_width]
    second_half = value[..., half_width:]
    return jnp.concatenate([first_half * cosine - second_half * sine, second_half * cosine + first_half * sine], axis=-1)

def gated_units(gate, up):
    return jax.nn.gelu(gate, approximate=True) * up

def attend(queries, keys, values, segment_ids):
    block_size = min(512, TOKENS)
    score_scale = HD ** (-0.5)
    padding = ((0, 0), (WINDOW, 0), (0, 0))
    key_padded = jnp.pad(keys, padding)
    value_padded = jnp.pad(values, padding)
    mark_padded = jnp.concatenate([jnp.full((WINDOW,), -1, jnp.int32), segment_ids.astype(jnp.int32)])
    distance = jnp.arange(block_size, dtype=jnp.int32)[:, None] + WINDOW - jnp.arange(block_size + WINDOW, dtype=jnp.int32)[None, :]
    inside = (distance >= 0) & (distance < WINDOW)

    @jax.checkpoint
    def one_block(start):
        query_block = lax.dynamic_slice_in_dim(queries, start, block_size, 1)
        key_block = lax.dynamic_slice_in_dim(key_padded, start, block_size + WINDOW, 1)
        value_block = lax.dynamic_slice_in_dim(value_padded, start, block_size + WINDOW, 1)
        query_marks = lax.dynamic_slice_in_dim(segment_ids, start, block_size, 0)
        key_marks = lax.dynamic_slice_in_dim(mark_padded, start, block_size + WINDOW, 0)
        visible = inside & (query_marks[:, None] == key_marks[None, :])
        scores = low_back(jnp.einsum('hqd,hkd->hqk', query_block, key_block, precision=HIGH) * score_scale)
        scores = jnp.where(visible[None], scores, NEG)
        highest = lax.optimization_barrier(jnp.max(scores, axis=-1, keepdims=True))
        expo = jnp.exp(scores - highest)
        probs = low(expo / lax.optimization_barrier(jnp.sum(expo, axis=-1, keepdims=True)))
        return jnp.einsum('hqk,hkd->hqd', probs, value_block, precision=HIGH)
    starts = jnp.arange(TOKENS // block_size, dtype=jnp.int32) * block_size
    blocks = lax.map(one_block, starts)
    return jnp.transpose(blocks, (1, 0, 2, 3)).reshape(queries.shape[0], TOKENS, queries.shape[2])

def block_forward(tokens, q_weight, kv_weight, o_weight, gate_up_weight, down_weight, attn_pre_gain, attn_post_gain, ff_pre_gain, ff_post_gain, query_gain, key_gain, segment_ids, cosine, sine):
    attn_in = low(normalize(tokens, attn_pre_gain))
    query_pre = low_back(jnp.dot(attn_in, q_weight, precision=HIGH))
    kv_pre = jnp.dot(attn_in, kv_weight, precision=HIGH)
    key_pre = low_back(jnp.broadcast_to(kv_pre[None, :, :HD], (HEADS, TOKENS, HD)))
    value_all = low(low_back(jnp.broadcast_to(kv_pre[None, :, HD:], (HEADS, TOKENS, HD))))
    query_heads = jnp.transpose(query_pre.reshape(TOKENS, HEADS, HD), (1, 0, 2))
    query_all = low(rotate(normalize(query_heads, query_gain), cosine, sine))
    key_all = low(rotate(normalize(key_pre, key_gain), cosine, sine))
    attended = low(low_back(attend(query_all, key_all, value_all, segment_ids)))
    attended_rows = jnp.transpose(attended, (1, 0, 2)).reshape(TOKENS, HEADS * HD)
    attn_out = low_back(jnp.dot(attended_rows, o_weight, precision=HIGH))
    middle = tokens + normalize(attn_out, attn_post_gain)
    ff_in = low(normalize(middle, ff_pre_gain))
    gate = low_back(jnp.dot(ff_in, gate_up_weight[0], precision=HIGH))
    up_part = low_back(jnp.dot(ff_in, gate_up_weight[1], precision=HIGH))
    hidden = low(gated_units(gate, up_part))
    ff_out = low_back(jnp.dot(hidden, down_weight, precision=HIGH))
    return middle + normalize(ff_out, ff_post_gain)

def reference(tokens, segment_ids, positions, q_weight, kv_weight, o_weight, gate_up_weight, down_weight, attn_pre_gain, attn_post_gain, ff_pre_gain, ff_post_gain, query_gain, key_gain, out_grad):
    cosine, sine = rotary_tables(positions, HD)
    floats = [item.astype(jnp.float32) for item in (tokens, q_weight, kv_weight, o_weight, gate_up_weight, down_weight, attn_pre_gain, attn_post_gain, ff_pre_gain, ff_post_gain, query_gain, key_gain)]

    def forward(*primals):
        return block_forward(*primals, segment_ids, cosine, sine)
    result, pull = jax.vjp(forward, *floats)
    grads = pull(out_grad.astype(jnp.float32))
    return (result.astype(jnp.bfloat16), grads[0], grads[1], grads[2], grads[3], grads[4], grads[5], grads[6], grads[7], grads[8], grads[9], grads[10], grads[11])
```

```python
from functools import partial

import jax
import jax.numpy as jnp
from jax import lax
from jax.sharding import PartitionSpec as P

WINDOW = 512


EPS = 1e-06
NEG = -1e30


def from_behind(value, axis, steps):
    count = lax.axis_size(axis)
    leading, last = (max(0, -steps), min(count, count - steps))
    return lax.ppermute(value, axis, [(source, source + steps) for source in range(leading, last)])


def shifted(value, axis, shift):
    count = lax.axis_size(axis)
    return lax.ppermute(value, axis, [(i, (i + shift) % count) for i in range(count)])


def gather_relative(value):
    count = lax.axis_size("mp")
    return [value] + [shifted(value, "mp", -step) for step in range(1, count)]


def gather_ordered(value):
    count = lax.axis_size("mp")
    rows = value.shape[0]
    me = lax.axis_index("mp")
    whole = jnp.zeros((count * rows,) + value.shape[1:], value.dtype)
    for step, block in enumerate(gather_relative(value)):
        owner = lax.rem(me + step, count)
        whole = lax.dynamic_update_slice_in_dim(whole, block, owner * rows, axis=0)
    return whole


def scatter_relative(blocks):
    total = blocks[0].astype(jnp.float32)
    for step in range(1, len(blocks)):
        total = total + shifted(blocks[step], "mp", step).astype(jnp.float32)
    return total


def scatter_ordered(value):
    count = lax.axis_size("mp")
    rows = value.shape[0] // count
    me = lax.axis_index("mp")
    return scatter_relative(
        [
            lax.dynamic_slice_in_dim(value, lax.rem(me + step, count) * rows, rows, axis=0)
            for step in range(count)
        ]
    )


def split_rows(value):
    rows = value.shape[0] // lax.axis_size("mp")
    return [value[i * rows : (i + 1) * rows] for i in range(lax.axis_size("mp"))]


def sum_over_mp(value):
    total = value.astype(jnp.float32)
    for step in range(1, lax.axis_size("mp")):
        total = total + shifted(value, "mp", step).astype(jnp.float32)
    return total


def normalize(value, gain):
    return value * lax.rsqrt(jnp.mean(value * value, axis=-1, keepdims=True) + EPS) * gain


def rotary_tables(positions, width):
    half_width = width // 2
    frequency = jnp.power(10000.0, -jnp.arange(half_width, dtype=jnp.float32) * (2.0 / width))
    angles = positions.astype(jnp.float32)[:, None] * frequency[None, :]
    return (jnp.cos(angles), jnp.sin(angles))


def rotate(value, cosine, sine):
    half_width = value.shape[-1] // 2
    first_half = value[..., :half_width]
    second_half = value[..., half_width:]
    return jnp.concatenate(
        [first_half * cosine - second_half * sine, second_half * cosine + first_half * sine],
        axis=-1,
    )


def prepare_head(pre_value, gain, cosine, sine):
    return rotate(normalize(pre_value, gain), cosine, sine)


def gated_units(gate, up_part):
    return jax.nn.gelu(gate, approximate=True) * up_part


def norm_back(value, gain, grad):
    unused, pull = jax.vjp(normalize, value, gain)
    return pull(grad)


def local(
    tokens,
    segment_ids,
    positions,
    q_weight,
    kv_weight,
    o_weight,
    gate_up_weight,
    down_weight,
    attn_pre_gain,
    attn_post_gain,
    ff_pre_gain,
    ff_post_gain,
    query_gain,
    key_gain,
    out_grad,
):
    rows = q_weight.shape[0]
    head_size = q_weight.shape[1]
    width = rows * lax.axis_size("dp")
    gain_rows = query_gain.shape[0]
    small_gains = [
        jnp.pad(item, (0, rows - gain_rows)) for item in (query_gain, key_gain)
    ]
    gain_columns = jnp.stack(
        [attn_pre_gain, attn_post_gain, ff_pre_gain, ff_post_gain] + small_gains, axis=1
    )
    gain_columns = jnp.pad(gain_columns, ((0, 0), (0, 128 - gain_columns.shape[1])))
    packed = jnp.concatenate(
        [q_weight, kv_weight, jnp.transpose(o_weight), gain_columns], axis=1
    )
    packed_full = lax.all_gather(packed, "dp", axis=0, tiled=True)
    gate_up_full = lax.all_gather(gate_up_weight, "dp", axis=1, tiled=True)
    down_full = lax.all_gather(down_weight, "dp", axis=1, tiled=True)
    joint_weight = packed_full[:, : 3 * head_size]
    output_turned = packed_full[:, 3 * head_size : 4 * head_size]
    gain_block = jnp.transpose(packed_full[:, 4 * head_size :]).astype(jnp.float32)
    gains = [gain_block[i] for i in range(4)] + [
        gain_block[i].reshape(-1, rows)[:, :gain_rows].reshape(-1) for i in (4, 5)
    ]
    length = segment_ids.shape[0]
    reach = -(-WINDOW // length)
    block_size = min(512, length)
    score_scale = head_size ** (-0.5)
    span = block_size + WINDOW
    cosine, sine = rotary_tables(positions, head_size)
    distance = (
        jnp.arange(block_size, dtype=jnp.int32)[:, None]
        + WINDOW
        - jnp.arange(span, dtype=jnp.int32)[None, :]
    )
    inside = (distance >= 0) & (distance < WINDOW)
    residual = tokens.astype(jnp.float32)
    attn_local = normalize(residual, gains[0]).astype(jnp.bfloat16)
    attn_in = gather_ordered(attn_local)
    projected = jnp.dot(attn_in, joint_weight, preferred_element_type=jnp.float32)
    query_pre = projected[:, :head_size]
    key_pre = projected[:, head_size : 2 * head_size]
    value_pre = projected[:, 2 * head_size :]
    queries = prepare_head(query_pre, gains[4], cosine, sine).astype(jnp.bfloat16)
    keys = prepare_head(key_pre, gains[5], cosine, sine).astype(jnp.bfloat16)
    values = value_pre.astype(jnp.bfloat16)
    marks = (segment_ids + 1).astype(jnp.bfloat16)
    key_parts, value_parts, mark_parts = ([], [], [])
    step = 1
    moved = from_behind((keys, values, marks), "dp", step)
    key_parts.append(moved[0])
    value_parts.append(moved[1])
    mark_parts.append(moved[2])
    all_keys = jnp.concatenate(key_parts + [keys], axis=0)
    all_values = jnp.concatenate(value_parts + [values], axis=0)
    all_marks = jnp.concatenate(mark_parts + [marks], axis=0)

    def block_parts(start):
        first_key = start + reach * length - WINDOW
        visible = inside & (marks[:, None] == all_marks[None, :])
        product = (
            jnp.einsum("qd,kd->qk", queries, all_keys, preferred_element_type=jnp.float32)
            * score_scale
        )
        return (first_key, queries, all_keys, all_values, jnp.where(visible, product, NEG))

    mixed_parts, total_parts = ([], [])
    start = 0
    first_key, query_block, key_block, value_block, scores = block_parts(start)
    highest = jnp.max(scores, axis=-1, keepdims=True)
    expo = jnp.exp(scores - highest)
    denominator = jnp.sum(expo, axis=-1, keepdims=True)
    probs = (expo / denominator).astype(jnp.bfloat16)
    mixed_parts.append(jnp.dot(probs, value_block, preferred_element_type=jnp.float32))
    total_parts.append(highest + jnp.log(denominator))
    attended = mixed_parts[0].astype(jnp.bfloat16)
    log_totals = total_parts[0]
    attn_out = scatter_ordered(
        jnp.einsum(
            "le,de->ld", attended, output_turned, preferred_element_type=jnp.float32
        ).astype(jnp.bfloat16)
    )
    middle = residual + normalize(attn_out, gains[1])
    ff_local = normalize(middle, gains[2]).astype(jnp.bfloat16)
    ff_in = jnp.concatenate(gather_relative(ff_local), axis=0)
    gate = jnp.dot(ff_in, gate_up_full[0], preferred_element_type=jnp.float32)
    up_part = jnp.dot(ff_in, gate_up_full[1], preferred_element_type=jnp.float32)
    hidden = gated_units(gate, up_part).astype(jnp.bfloat16)
    ff_out = scatter_relative(
        split_rows(
            jnp.dot(hidden, down_full, preferred_element_type=jnp.float32).astype(jnp.bfloat16)
        )
    )
    result = (middle + normalize(ff_out, gains[3])).astype(jnp.bfloat16)
    top_grad = out_grad.astype(jnp.float32)
    ff_out_grad, ff_post_grad = norm_back(ff_out, gains[3], top_grad)
    ff_grad_all = jnp.concatenate(gather_relative(ff_out_grad.astype(jnp.bfloat16)), axis=0)
    hidden_grad = jnp.einsum(
        "ld,fd->lf", ff_grad_all, down_full, preferred_element_type=jnp.float32
    )
    down_grad_turned = jnp.einsum(
        "ld,lf->df", ff_grad_all, hidden, preferred_element_type=jnp.float32
    )
    unused, unit_pull = jax.vjp(gated_units, gate, up_part)
    gate_grad, up_grad = unit_pull(hidden_grad)
    gate_low = gate_grad.astype(jnp.bfloat16)
    up_low = up_grad.astype(jnp.bfloat16)
    gate_turned = jnp.einsum("ld,lf->df", ff_in, gate_low, preferred_element_type=jnp.float32)
    up_turned = jnp.einsum("ld,lf->df", ff_in, up_low, preferred_element_type=jnp.float32)
    ff_in_partial = (
        jnp.einsum("lf,df->ld", gate_low, gate_up_full[0], preferred_element_type=jnp.float32)
        + jnp.einsum("lf,df->ld", up_low, gate_up_full[1], preferred_element_type=jnp.float32)
    ).astype(jnp.bfloat16)
    ff_in_partial, down_low, gate_turned_low, up_turned_low = lax.optimization_barrier(
        (
            ff_in_partial,
            down_grad_turned.astype(jnp.bfloat16),
            gate_turned.astype(jnp.bfloat16),
            up_turned.astype(jnp.bfloat16),
        )
    )
    feed_forward_owned = tuple(
        lax.psum_scatter(item, "dp", scatter_dimension=0, tiled=True)
        for item in (down_low, gate_turned_low, up_turned_low)
    )
    ff_in_grad = scatter_relative(split_rows(ff_in_partial))
    middle_part, ff_pre_grad = norm_back(middle, gains[2], ff_in_grad)
    middle_grad = top_grad + middle_part
    attn_out_grad, attn_post_grad = norm_back(attn_out, gains[1], middle_grad)
    attn_grad_all = gather_ordered(attn_out_grad.astype(jnp.bfloat16))
    attended_grad = jnp.einsum(
        "ld,de->le", attn_grad_all, output_turned, preferred_element_type=jnp.float32
    ).astype(jnp.bfloat16)
    output_grad_turned = jnp.einsum(
        "ld,le->de", attn_grad_all, attended, preferred_element_type=jnp.float32
    )
    key_grad_all = jnp.zeros(((reach + 1) * length, head_size), jnp.float32)
    value_grad_all = jnp.zeros(((reach + 1) * length, head_size), jnp.float32)
    start = 0
    first_key, query_block, key_block, value_block, scores = block_parts(start)
    probs = jnp.exp(scores - log_totals)
    probs_low = probs.astype(jnp.bfloat16)
    value_grad_all = value_grad_all.at[first_key : first_key + span].add(
        jnp.einsum("qk,qd->kd", probs_low, attended_grad, preferred_element_type=jnp.float32)
    )
    prob_grad = jnp.einsum(
        "qd,kd->qk", attended_grad, value_block, preferred_element_type=jnp.float32
    )
    inner = jnp.sum(probs * prob_grad, axis=-1, keepdims=True)
    score_grad = (probs * (prob_grad - inner)).astype(jnp.bfloat16)
    query_parts = jnp.dot(score_grad, key_block, preferred_element_type=jnp.float32) * score_scale
    key_grad_all = key_grad_all.at[first_key : first_key + span].add(
        jnp.einsum("qk,qd->kd", score_grad, query_block, preferred_element_type=jnp.float32)
        * score_scale
    )
    own_keys = key_grad_all[reach * length :]
    own_values = value_grad_all[reach * length :]
    step = 1
    slot = reach - step
    returned = (
        from_behind(
            key_grad_all[slot * length : (slot + 1) * length].astype(jnp.bfloat16), "dp", -step
        ).astype(jnp.float32),
        from_behind(
            value_grad_all[slot * length : (slot + 1) * length].astype(jnp.bfloat16), "dp", -step
        ).astype(jnp.float32),
    )
    own_keys = own_keys + returned[0]
    own_values = own_values + returned[1]
    unused, query_pull = jax.vjp(
        partial(prepare_head, cosine=cosine, sine=sine), query_pre, gains[4]
    )
    query_pre_grad, query_gain_grad = query_pull(query_parts)
    unused, key_pull = jax.vjp(
        partial(prepare_head, cosine=cosine, sine=sine), key_pre, gains[5]
    )
    key_pre_grad, key_gain_grad = key_pull(own_keys)
    joint_grad_rows = jnp.concatenate([query_pre_grad, key_pre_grad, own_values], axis=1).astype(
        jnp.bfloat16
    )
    joint_grad = jnp.einsum(
        "ld,lc->dc", attn_in, joint_grad_rows, preferred_element_type=jnp.float32
    )
    attn_in_grad = scatter_ordered(
        jnp.einsum(
            "lc,dc->ld", joint_grad_rows, joint_weight, preferred_element_type=jnp.float32
        ).astype(jnp.bfloat16)
    )
    tokens_part, attn_pre_grad = norm_back(residual, gains[0], attn_in_grad)
    tokens_grad = middle_grad + tokens_part
    small_grads = [
        jnp.pad(item.reshape(-1, gain_rows), ((0, 0), (0, rows - gain_rows))).reshape(-1)
        for item in (query_gain_grad, key_gain_grad)
    ]
    gain_grads = jnp.stack(
        [attn_pre_grad, attn_post_grad, ff_pre_grad, ff_post_grad] + small_grads, axis=1
    )
    gain_grads = jnp.pad(gain_grads, ((0, 0), (0, 128 - gain_grads.shape[1])))
    packed_grad = jnp.concatenate(
        [
            joint_grad[:, :head_size].astype(jnp.bfloat16),
            output_grad_turned.astype(jnp.bfloat16),
            joint_grad[:, head_size:].astype(jnp.bfloat16),
            gain_grads.astype(jnp.bfloat16),
        ],
        axis=1,
    )
    packed_grad, feed_forward_owned = lax.optimization_barrier(
        (packed_grad, feed_forward_owned)
    )
    down_owned = jnp.transpose(feed_forward_owned[0]).astype(jnp.float32)
    gate_up_owned = jnp.stack(feed_forward_owned[1:], axis=0).astype(jnp.float32)
    packed_owned = lax.psum_scatter(packed_grad, "dp", scatter_dimension=0, tiled=True)
    query_owned = packed_owned[:, :head_size].astype(jnp.float32)
    output_owned = jnp.transpose(packed_owned[:, head_size : 2 * head_size]).astype(jnp.float32)
    summed = sum_over_mp(packed_owned[:, 2 * head_size :])
    keyval_owned = summed[:, : 2 * head_size]
    gain_owned = jnp.transpose(summed[:, 2 * head_size :])
    return (
        result,
        tokens_grad,
        query_owned,
        keyval_owned,
        output_owned,
        gate_up_owned,
        down_owned,
        gain_owned[0],
        gain_owned[1],
        gain_owned[2],
        gain_owned[3],
        gain_owned[4, :gain_rows],
        gain_owned[5, :gain_rows],
    )


def solution(mesh):
    placed = (
        P(("dp", "mp"), None),
        P("dp"),
        P("dp"),
        P("dp", "mp"),
        P("dp", None),
        P("mp", "dp"),
        P(None, "dp", "mp"),
        P("mp", "dp"),
        P("dp"),
        P("dp"),
        P("dp"),
        P("dp"),
        P("dp"),
        P("dp"),
        P(("dp", "mp"), None),
    )
    return jax.shard_map(
        local,
        mesh=mesh,
        in_specs=placed,
        out_specs=(
            P(("dp", "mp"), None),
            P(("dp", "mp"), None),
            P("dp", "mp"),
            P("dp", None),
            P("mp", "dp"),
            P(None, "dp", "mp"),
            P("mp", "dp"),
            P("dp"),
            P("dp"),
            P("dp"),
            P("dp"),
            P("dp"),
            P("dp"),
        ),
        check_vma=False,
    )
```

```python
from functools import partial

import jax
import jax.numpy as jnp
from jax import lax
from jax.sharding import PartitionSpec as P

WINDOW = 512


EPS = 1e-06
NEG = -1e30


def from_behind(value, axis, steps):
    count = lax.axis_size(axis)
    leading, last = (max(0, -steps), min(count, count - steps))
    return lax.ppermute(value, axis, [(source, source + steps) for source in range(leading, last)])


def shifted(value, axis, shift):
    count = lax.axis_size(axis)
    return lax.ppermute(value, axis, [(i, (i + shift) % count) for i in range(count)])


def gather_relative(value):
    count = lax.axis_size("mp")
    return [value] + [shifted(value, "mp", -step) for step in range(1, count)]


def gather_ordered(value):
    count = lax.axis_size("mp")
    rows = value.shape[0]
    me = lax.axis_index("mp")
    whole = jnp.zeros((count * rows,) + value.shape[1:], value.dtype)
    for step, block in enumerate(gather_relative(value)):
        owner = lax.rem(me + step, count)
        whole = lax.dynamic_update_slice_in_dim(whole, block, owner * rows, axis=0)
    return whole


def scatter_relative(blocks):
    total = blocks[0].astype(jnp.float32)
    for step in range(1, len(blocks)):
        total = total + shifted(blocks[step], "mp", step).astype(jnp.float32)
    return total


def scatter_ordered(value):
    count = lax.axis_size("mp")
    rows = value.shape[0] // count
    me = lax.axis_index("mp")
    return scatter_relative(
        [
            lax.dynamic_slice_in_dim(value, lax.rem(me + step, count) * rows, rows, axis=0)
            for step in range(count)
        ]
    )


def swap_pairs(value):
    count = lax.axis_size("dp")
    return lax.ppermute(value, "dp", [(i, i + 1 - 2 * (i % 2)) for i in range(count)])


def gather_dp(value):
    half = lax.axis_size("dp") // 2
    me = lax.axis_index("dp")
    other = swap_pairs(value)
    pair = jnp.where(
        lax.rem(me, 2) == 0,
        jnp.concatenate([value, other], axis=0),
        jnp.concatenate([other, value], axis=0),
    )
    rows = pair.shape[0]
    whole = jnp.zeros((half * rows,) + value.shape[1:], value.dtype)
    for step in range(half):
        block = pair if step == 0 else shifted(pair, "dp", -2 * step)
        owner = lax.rem(me // 2 + step, half)
        whole = lax.dynamic_update_slice_in_dim(whole, block, owner * rows, axis=0)
    return whole


def scatter_dp(value):
    half = lax.axis_size("dp") // 2
    me = lax.axis_index("dp")
    parity = lax.rem(me, 2)
    split = value.reshape((half, 2, -1) + value.shape[1:])
    kept = lax.dynamic_index_in_dim(split, parity, axis=1, keepdims=False)
    sent = lax.dynamic_index_in_dim(split, 1 - parity, axis=1, keepdims=False)
    part = kept.astype(jnp.float32) + swap_pairs(sent).astype(jnp.float32)
    blocks = [
        lax.dynamic_index_in_dim(part, lax.rem(me // 2 + step, half), axis=0, keepdims=False)
        for step in range(half)
    ]
    total = blocks[0]
    for step in range(1, half):
        total = total + shifted(blocks[step].astype(value.dtype), "dp", 2 * step).astype(
            jnp.float32
        )
    return total


def split_rows(value):
    rows = value.shape[0] // lax.axis_size("mp")
    return [value[i * rows : (i + 1) * rows] for i in range(lax.axis_size("mp"))]


def sum_over_mp(value):
    total = value.astype(jnp.float32)
    for step in range(1, lax.axis_size("mp")):
        total = total + shifted(value, "mp", step).astype(jnp.float32)
    return total


def normalize(value, gain):
    return value * lax.rsqrt(jnp.mean(value * value, axis=-1, keepdims=True) + EPS) * gain


def rotary_tables(positions, width):
    half_width = width // 2
    frequency = jnp.power(10000.0, -jnp.arange(half_width, dtype=jnp.float32) * (2.0 / width))
    angles = positions.astype(jnp.float32)[:, None] * frequency[None, :]
    return (jnp.cos(angles), jnp.sin(angles))


def rotate(value, cosine, sine):
    half_width = value.shape[-1] // 2
    first_half = value[..., :half_width]
    second_half = value[..., half_width:]
    return jnp.concatenate(
        [first_half * cosine - second_half * sine, second_half * cosine + first_half * sine],
        axis=-1,
    )


def prepare_head(pre_value, gain, cosine, sine):
    return rotate(normalize(pre_value, gain), cosine, sine)


def gated_units(gate, up_part):
    return jax.nn.gelu(gate, approximate=True) * up_part


def norm_back(value, gain, grad):
    unused, pull = jax.vjp(normalize, value, gain)
    return pull(grad)


def local(
    tokens,
    segment_ids,
    positions,
    q_weight,
    kv_weight,
    o_weight,
    gate_up_weight,
    down_weight,
    attn_pre_gain,
    attn_post_gain,
    ff_pre_gain,
    ff_post_gain,
    query_gain,
    key_gain,
    out_grad,
):
    rows = q_weight.shape[0]
    head_size = q_weight.shape[1]
    width = rows * lax.axis_size("dp")
    gain_rows = query_gain.shape[0]
    small_gains = [
        jnp.pad(item, (0, rows - gain_rows)) for item in (query_gain, key_gain)
    ]
    gain_columns = jnp.stack(
        [attn_pre_gain, attn_post_gain, ff_pre_gain, ff_post_gain] + small_gains, axis=1
    )
    gain_columns = jnp.pad(gain_columns, ((0, 0), (0, 128 - gain_columns.shape[1])))
    packed = jnp.concatenate(
        [q_weight, kv_weight, jnp.transpose(o_weight), gain_columns], axis=1
    )
    packed_full = gather_dp(packed)
    gate_up_full = lax.all_gather(gate_up_weight, "dp", axis=1, tiled=True)
    down_turned = gather_dp(jnp.transpose(down_weight))
    joint_weight = packed_full[:, : 3 * head_size]
    output_turned = packed_full[:, 3 * head_size : 4 * head_size]
    gain_block = jnp.transpose(packed_full[:, 4 * head_size :]).astype(jnp.float32)
    gains = [gain_block[i] for i in range(4)] + [
        gain_block[i].reshape(-1, rows)[:, :gain_rows].reshape(-1) for i in (4, 5)
    ]
    length = segment_ids.shape[0]
    reach = -(-WINDOW // length)
    block_size = min(512, length)
    score_scale = head_size ** (-0.5)
    span = block_size + WINDOW
    cosine, sine = rotary_tables(positions, head_size)
    distance = (
        jnp.arange(block_size, dtype=jnp.int32)[:, None]
        + WINDOW
        - jnp.arange(span, dtype=jnp.int32)[None, :]
    )
    inside = (distance >= 0) & (distance < WINDOW)
    residual = tokens.astype(jnp.float32)
    attn_local = normalize(residual, gains[0]).astype(jnp.bfloat16)
    attn_in = gather_ordered(attn_local)
    projected = jnp.dot(attn_in, joint_weight, preferred_element_type=jnp.float32)
    query_pre = projected[:, :head_size]
    key_pre = projected[:, head_size : 2 * head_size]
    value_pre = projected[:, 2 * head_size :]
    queries = prepare_head(query_pre, gains[4], cosine, sine).astype(jnp.bfloat16)
    keys = prepare_head(key_pre, gains[5], cosine, sine).astype(jnp.bfloat16)
    values = value_pre.astype(jnp.bfloat16)
    marks = (segment_ids + 1).astype(jnp.bfloat16)
    key_parts, value_parts, mark_parts = ([], [], [])
    step = 1
    moved = from_behind((keys, values, marks), "dp", step)
    key_parts.append(moved[0])
    value_parts.append(moved[1])
    mark_parts.append(moved[2])
    all_keys = jnp.concatenate(key_parts + [keys], axis=0)
    all_values = jnp.concatenate(value_parts + [values], axis=0)
    all_marks = jnp.concatenate(mark_parts + [marks], axis=0)

    def block_parts(start):
        first_key = start + reach * length - WINDOW
        visible = inside & (marks[:, None] == all_marks[None, :])
        product = (
            jnp.einsum("qd,kd->qk", queries, all_keys, preferred_element_type=jnp.float32)
            * score_scale
        )
        return (first_key, queries, all_keys, all_values, jnp.where(visible, product, NEG))

    mixed_parts, total_parts = ([], [])
    start = 0
    first_key, query_block, key_block, value_block, scores = block_parts(start)
    highest = jnp.max(scores, axis=-1, keepdims=True)
    expo = jnp.exp(scores - highest)
    denominator = jnp.sum(expo, axis=-1, keepdims=True)
    probs = (expo / denominator).astype(jnp.bfloat16)
    mixed_parts.append(jnp.dot(probs, value_block, preferred_element_type=jnp.float32))
    total_parts.append(highest + jnp.log(denominator))
    attended = mixed_parts[0].astype(jnp.bfloat16)
    log_totals = total_parts[0]
    attn_out = scatter_ordered(
        jnp.einsum(
            "le,de->ld", attended, output_turned, preferred_element_type=jnp.float32
        ).astype(jnp.bfloat16)
    )
    middle = residual + normalize(attn_out, gains[1])
    ff_local = normalize(middle, gains[2]).astype(jnp.bfloat16)
    ff_in = jnp.concatenate(gather_relative(ff_local), axis=0)
    gate = jnp.dot(ff_in, gate_up_full[0], preferred_element_type=jnp.float32)
    up_part = jnp.dot(ff_in, gate_up_full[1], preferred_element_type=jnp.float32)
    hidden = gated_units(gate, up_part).astype(jnp.bfloat16)
    ff_out = scatter_relative(
        split_rows(
            jnp.einsum(
                "lf,df->ld", hidden, down_turned, preferred_element_type=jnp.float32
            ).astype(jnp.bfloat16)
        )
    )
    result = (middle + normalize(ff_out, gains[3])).astype(jnp.bfloat16)
    top_grad = out_grad.astype(jnp.float32)
    ff_out_grad, ff_post_grad = norm_back(ff_out, gains[3], top_grad)
    ff_grad_all = jnp.concatenate(gather_relative(ff_out_grad.astype(jnp.bfloat16)), axis=0)
    down_low = jnp.einsum(
        "ld,lf->df", ff_grad_all, hidden, preferred_element_type=jnp.float32
    ).astype(jnp.bfloat16)
    ff_grad_all, down_low = lax.optimization_barrier((ff_grad_all, down_low))
    hidden_grad = jnp.einsum(
        "ld,df->lf", ff_grad_all, down_turned, preferred_element_type=jnp.float32
    )
    unused, unit_pull = jax.vjp(gated_units, gate, up_part)
    gate_grad, up_grad = unit_pull(hidden_grad)
    gate_low = gate_grad.astype(jnp.bfloat16)
    up_low = up_grad.astype(jnp.bfloat16)
    gate_turned = jnp.einsum("ld,lf->df", ff_in, gate_low, preferred_element_type=jnp.float32)
    up_turned = jnp.einsum("ld,lf->df", ff_in, up_low, preferred_element_type=jnp.float32)
    ff_in_partial = (
        jnp.einsum("lf,df->ld", gate_low, gate_up_full[0], preferred_element_type=jnp.float32)
        + jnp.einsum("lf,df->ld", up_low, gate_up_full[1], preferred_element_type=jnp.float32)
    ).astype(jnp.bfloat16)
    ff_in_partial, gate_turned_low, up_turned_low = lax.optimization_barrier(
        (
            ff_in_partial,
            gate_turned.astype(jnp.bfloat16),
            up_turned.astype(jnp.bfloat16),
        )
    )
    gate_up_parts = tuple(
        lax.psum_scatter(item, "dp", scatter_dimension=0, tiled=True)
        for item in (gate_turned_low, up_turned_low)
    )
    ff_in_grad = scatter_relative(split_rows(ff_in_partial))
    middle_part, ff_pre_grad = norm_back(middle, gains[2], ff_in_grad)
    middle_grad = top_grad + middle_part
    attn_out_grad, attn_post_grad = norm_back(attn_out, gains[1], middle_grad)
    attn_grad_all = gather_ordered(attn_out_grad.astype(jnp.bfloat16))
    attended_grad = jnp.einsum(
        "ld,de->le", attn_grad_all, output_turned, preferred_element_type=jnp.float32
    ).astype(jnp.bfloat16)
    output_grad_turned = jnp.einsum(
        "ld,le->de", attn_grad_all, attended, preferred_element_type=jnp.float32
    )
    key_grad_all = jnp.zeros(((reach + 1) * length, head_size), jnp.float32)
    value_grad_all = jnp.zeros(((reach + 1) * length, head_size), jnp.float32)
    start = 0
    first_key, query_block, key_block, value_block, scores = block_parts(start)
    probs = jnp.exp(scores - log_totals)
    probs_low = probs.astype(jnp.bfloat16)
    value_grad_all = value_grad_all.at[first_key : first_key + span].add(
        jnp.einsum("qk,qd->kd", probs_low, attended_grad, preferred_element_type=jnp.float32)
    )
    prob_grad = jnp.einsum(
        "qd,kd->qk", attended_grad, value_block, preferred_element_type=jnp.float32
    )
    inner = jnp.sum(probs * prob_grad, axis=-1, keepdims=True)
    score_grad = (probs * (prob_grad - inner)).astype(jnp.bfloat16)
    query_parts = jnp.dot(score_grad, key_block, preferred_element_type=jnp.float32) * score_scale
    key_grad_all = key_grad_all.at[first_key : first_key + span].add(
        jnp.einsum("qk,qd->kd", score_grad, query_block, preferred_element_type=jnp.float32)
        * score_scale
    )
    own_keys = key_grad_all[reach * length :]
    own_values = value_grad_all[reach * length :]
    step = 1
    slot = reach - step
    returned = (
        from_behind(
            key_grad_all[slot * length : (slot + 1) * length].astype(jnp.bfloat16), "dp", -step
        ).astype(jnp.float32),
        from_behind(
            value_grad_all[slot * length : (slot + 1) * length].astype(jnp.bfloat16), "dp", -step
        ).astype(jnp.float32),
    )
    own_keys = own_keys + returned[0]
    own_values = own_values + returned[1]
    unused, query_pull = jax.vjp(
        partial(prepare_head, cosine=cosine, sine=sine), query_pre, gains[4]
    )
    query_pre_grad, query_gain_grad = query_pull(query_parts)
    unused, key_pull = jax.vjp(
        partial(prepare_head, cosine=cosine, sine=sine), key_pre, gains[5]
    )
    key_pre_grad, key_gain_grad = key_pull(own_keys)
    joint_grad_rows = jnp.concatenate([query_pre_grad, key_pre_grad, own_values], axis=1).astype(
        jnp.bfloat16
    )
    joint_grad = jnp.einsum(
        "ld,lc->dc", attn_in, joint_grad_rows, preferred_element_type=jnp.float32
    )
    attn_in_grad = scatter_ordered(
        jnp.einsum(
            "lc,dc->ld", joint_grad_rows, joint_weight, preferred_element_type=jnp.float32
        ).astype(jnp.bfloat16)
    )
    tokens_part, attn_pre_grad = norm_back(residual, gains[0], attn_in_grad)
    tokens_grad = middle_grad + tokens_part
    small_grads = [
        jnp.pad(item.reshape(-1, gain_rows), ((0, 0), (0, rows - gain_rows))).reshape(-1)
        for item in (query_gain_grad, key_gain_grad)
    ]
    gain_grads = jnp.stack(
        [attn_pre_grad, attn_post_grad, ff_pre_grad, ff_post_grad] + small_grads, axis=1
    )
    gain_grads = jnp.pad(gain_grads, ((0, 0), (0, 128 - gain_grads.shape[1])))
    packed_grad = jnp.concatenate(
        [
            joint_grad[:, :head_size].astype(jnp.bfloat16),
            output_grad_turned.astype(jnp.bfloat16),
            joint_grad[:, head_size:].astype(jnp.bfloat16),
            gain_grads.astype(jnp.bfloat16),
        ],
        axis=1,
    )
    down_owned = jnp.transpose(scatter_dp(down_low))
    gate_up_owned = jnp.stack(gate_up_parts, axis=0).astype(jnp.float32)
    packed_owned = scatter_dp(packed_grad)
    query_owned = packed_owned[:, :head_size].astype(jnp.float32)
    output_owned = jnp.transpose(packed_owned[:, head_size : 2 * head_size]).astype(jnp.float32)
    summed = sum_over_mp(packed_owned[:, 2 * head_size :].astype(jnp.bfloat16))
    keyval_owned = summed[:, : 2 * head_size]
    gain_owned = jnp.transpose(summed[:, 2 * head_size :])
    return (
        result,
        tokens_grad,
        query_owned,
        keyval_owned,
        output_owned,
        gate_up_owned,
        down_owned,
        gain_owned[0],
        gain_owned[1],
        gain_owned[2],
        gain_owned[3],
        gain_owned[4, :gain_rows],
        gain_owned[5, :gain_rows],
    )


def solution(mesh):
    placed = (
        P(("dp", "mp"), None),
        P("dp"),
        P("dp"),
        P("dp", "mp"),
        P("dp", None),
        P("mp", "dp"),
        P(None, "dp", "mp"),
        P("mp", "dp"),
        P("dp"),
        P("dp"),
        P("dp"),
        P("dp"),
        P("dp"),
        P("dp"),
        P(("dp", "mp"), None),
    )
    return jax.shard_map(
        local,
        mesh=mesh,
        in_specs=placed,
        out_specs=(
            P(("dp", "mp"), None),
            P(("dp", "mp"), None),
            P("dp", "mp"),
            P("dp", None),
            P("mp", "dp"),
            P(None, "dp", "mp"),
            P("mp", "dp"),
            P("dp"),
            P("dp"),
            P("dp"),
            P("dp"),
            P("dp"),
            P("dp"),
        ),
        check_vma=False,
    )
```

```python
from functools import partial

import jax
import jax.numpy as jnp
from jax import lax
from jax.sharding import PartitionSpec as P

WINDOW = 512


EPS = 1e-06
NEG = -1e30


def from_behind(value, axis, steps):
    count = lax.axis_size(axis)
    leading, last = (max(0, -steps), min(count, count - steps))
    return lax.ppermute(value, axis, [(source, source + steps) for source in range(leading, last)])


def shifted(value, axis, shift):
    count = lax.axis_size(axis)
    return lax.ppermute(value, axis, [(i, (i + shift) % count) for i in range(count)])


def gather_relative(value):
    count = lax.axis_size("mp")
    return [value] + [shifted(value, "mp", -step) for step in range(1, count)]


def gather_ordered(value):
    count = lax.axis_size("mp")
    rows = value.shape[0]
    me = lax.axis_index("mp")
    whole = jnp.zeros((count * rows,) + value.shape[1:], value.dtype)
    for step, block in enumerate(gather_relative(value)):
        owner = lax.rem(me + step, count)
        whole = lax.dynamic_update_slice_in_dim(whole, block, owner * rows, axis=0)
    return whole


def scatter_relative(blocks):
    total = blocks[0].astype(jnp.float32)
    for step in range(1, len(blocks)):
        total = total + shifted(blocks[step], "mp", step).astype(jnp.float32)
    return total


def scatter_ordered(value):
    count = lax.axis_size("mp")
    rows = value.shape[0] // count
    me = lax.axis_index("mp")
    return scatter_relative(
        [
            lax.dynamic_slice_in_dim(value, lax.rem(me + step, count) * rows, rows, axis=0)
            for step in range(count)
        ]
    )


def swap_pairs(value):
    count = lax.axis_size("dp")
    return lax.ppermute(value, "dp", [(i, i + 1 - 2 * (i % 2)) for i in range(count)])


def scatter_dp(value):
    half = lax.axis_size("dp") // 2
    me = lax.axis_index("dp")
    parity = lax.rem(me, 2)
    split = value.reshape((half, 2, -1) + value.shape[1:])
    kept = lax.dynamic_index_in_dim(split, parity, axis=1, keepdims=False)
    sent = lax.dynamic_index_in_dim(split, 1 - parity, axis=1, keepdims=False)
    part = kept.astype(jnp.float32) + swap_pairs(sent).astype(jnp.float32)
    blocks = [
        lax.dynamic_index_in_dim(part, lax.rem(me // 2 + step, half), axis=0, keepdims=False)
        for step in range(half)
    ]
    total = blocks[0]
    for step in range(1, half):
        total = total + shifted(blocks[step].astype(value.dtype), "dp", 2 * step).astype(
            jnp.float32
        )
    return total


def split_rows(value):
    rows = value.shape[0] // lax.axis_size("mp")
    return [value[i * rows : (i + 1) * rows] for i in range(lax.axis_size("mp"))]


def sum_over_mp(value):
    total = value.astype(jnp.float32)
    for step in range(1, lax.axis_size("mp")):
        total = total + shifted(value, "mp", step).astype(jnp.float32)
    return total


def normalize(value, gain):
    return value * lax.rsqrt(jnp.mean(value * value, axis=-1, keepdims=True) + EPS) * gain


def rotary_tables(positions, width):
    half_width = width // 2
    frequency = jnp.power(10000.0, -jnp.arange(half_width, dtype=jnp.float32) * (2.0 / width))
    angles = positions.astype(jnp.float32)[:, None] * frequency[None, :]
    return (jnp.cos(angles), jnp.sin(angles))


def rotate(value, cosine, sine):
    half_width = value.shape[-1] // 2
    first_half = value[..., :half_width]
    second_half = value[..., half_width:]
    return jnp.concatenate(
        [first_half * cosine - second_half * sine, second_half * cosine + first_half * sine],
        axis=-1,
    )


def prepare_head(pre_value, gain, cosine, sine):
    return rotate(normalize(pre_value, gain), cosine, sine)


def gated_units(gate, up_part):
    return jax.nn.gelu(gate, approximate=True) * up_part


def norm_back(value, gain, grad):
    unused, pull = jax.vjp(normalize, value, gain)
    return pull(grad)


def local(
    tokens,
    segment_ids,
    positions,
    q_weight,
    kv_weight,
    o_weight,
    gate_up_weight,
    down_weight,
    attn_pre_gain,
    attn_post_gain,
    ff_pre_gain,
    ff_post_gain,
    query_gain,
    key_gain,
    out_grad,
):
    rows = q_weight.shape[0]
    head_size = q_weight.shape[1]
    width = rows * lax.axis_size("dp")
    gain_rows = query_gain.shape[0]
    small_gains = [
        jnp.pad(item, (0, rows - gain_rows)) for item in (query_gain, key_gain)
    ]
    gain_columns = jnp.stack(
        [attn_pre_gain, attn_post_gain, ff_pre_gain, ff_post_gain] + small_gains, axis=1
    )
    gain_columns = jnp.pad(gain_columns, ((0, 0), (0, 128 - gain_columns.shape[1])))
    packed = jnp.concatenate(
        [q_weight, kv_weight, jnp.transpose(o_weight), gain_columns], axis=1
    )
    packed_full = lax.all_gather(packed, "dp", axis=0, tiled=True)
    gate_up_full = lax.all_gather(gate_up_weight, "dp", axis=1, tiled=True)
    down_full = lax.all_gather(down_weight, "dp", axis=1, tiled=True)
    joint_weight = packed_full[:, : 3 * head_size]
    output_turned = packed_full[:, 3 * head_size : 4 * head_size]
    gain_block = jnp.transpose(packed_full[:, 4 * head_size :]).astype(jnp.float32)
    gains = [gain_block[i] for i in range(4)] + [
        gain_block[i].reshape(-1, rows)[:, :gain_rows].reshape(-1) for i in (4, 5)
    ]
    length = segment_ids.shape[0]
    reach = -(-WINDOW // length)
    block_size = min(512, length)
    score_scale = head_size ** (-0.5)
    span = block_size + WINDOW
    cosine, sine = rotary_tables(positions, head_size)
    distance = (
        jnp.arange(block_size, dtype=jnp.int32)[:, None]
        + WINDOW
        - jnp.arange(span, dtype=jnp.int32)[None, :]
    )
    inside = (distance >= 0) & (distance < WINDOW)
    residual = tokens.astype(jnp.float32)
    attn_local = normalize(residual, gains[0]).astype(jnp.bfloat16)
    attn_in = gather_ordered(attn_local)
    projected = jnp.dot(attn_in, joint_weight, preferred_element_type=jnp.float32)
    query_pre = projected[:, :head_size]
    key_pre = projected[:, head_size : 2 * head_size]
    value_pre = projected[:, 2 * head_size :]
    queries = prepare_head(query_pre, gains[4], cosine, sine).astype(jnp.bfloat16)
    keys = prepare_head(key_pre, gains[5], cosine, sine).astype(jnp.bfloat16)
    values = value_pre.astype(jnp.bfloat16)
    marks = (segment_ids + 1).astype(jnp.bfloat16)
    key_parts, value_parts, mark_parts = ([], [], [])
    step = 1
    moved = from_behind((keys, values, marks), "dp", step)
    key_parts.append(moved[0])
    value_parts.append(moved[1])
    mark_parts.append(moved[2])
    all_keys = jnp.concatenate(key_parts + [keys], axis=0)
    all_values = jnp.concatenate(value_parts + [values], axis=0)
    all_marks = jnp.concatenate(mark_parts + [marks], axis=0)

    def block_parts(start):
        first_key = start + reach * length - WINDOW
        visible = inside & (marks[:, None] == all_marks[None, :])
        product = (
            jnp.einsum("qd,kd->qk", queries, all_keys, preferred_element_type=jnp.float32)
            * score_scale
        )
        return (first_key, queries, all_keys, all_values, jnp.where(visible, product, NEG))

    mixed_parts, total_parts = ([], [])
    start = 0
    first_key, query_block, key_block, value_block, scores = block_parts(start)
    highest = jnp.max(scores, axis=-1, keepdims=True)
    expo = jnp.exp(scores - highest)
    denominator = jnp.sum(expo, axis=-1, keepdims=True)
    probs = (expo / denominator).astype(jnp.bfloat16)
    mixed_parts.append(jnp.dot(probs, value_block, preferred_element_type=jnp.float32))
    total_parts.append(highest + jnp.log(denominator))
    attended = mixed_parts[0].astype(jnp.bfloat16)
    log_totals = total_parts[0]
    attn_out = scatter_ordered(
        jnp.einsum(
            "le,de->ld", attended, output_turned, preferred_element_type=jnp.float32
        ).astype(jnp.bfloat16)
    )
    middle = residual + normalize(attn_out, gains[1])
    ff_local = normalize(middle, gains[2]).astype(jnp.bfloat16)
    ff_in = jnp.concatenate(gather_relative(ff_local), axis=0)
    gate = jnp.dot(ff_in, gate_up_full[0], preferred_element_type=jnp.float32)
    up_part = jnp.dot(ff_in, gate_up_full[1], preferred_element_type=jnp.float32)
    hidden = gated_units(gate, up_part).astype(jnp.bfloat16)
    ff_out = scatter_relative(
        split_rows(
            jnp.dot(hidden, down_full, preferred_element_type=jnp.float32).astype(jnp.bfloat16)
        )
    )
    result = (middle + normalize(ff_out, gains[3])).astype(jnp.bfloat16)
    top_grad = out_grad.astype(jnp.float32)
    ff_out_grad, ff_post_grad = norm_back(ff_out, gains[3], top_grad)
    ff_grad_all = jnp.concatenate(gather_relative(ff_out_grad.astype(jnp.bfloat16)), axis=0)
    down_low = jnp.einsum(
        "ld,lf->df", ff_grad_all, hidden, preferred_element_type=jnp.float32
    ).astype(jnp.bfloat16)
    ff_grad_all, down_low = lax.optimization_barrier((ff_grad_all, down_low))
    hidden_grad = jnp.einsum(
        "ld,fd->lf", ff_grad_all, down_full, preferred_element_type=jnp.float32
    )
    unused, unit_pull = jax.vjp(gated_units, gate, up_part)
    gate_grad, up_grad = unit_pull(hidden_grad)
    gate_low = gate_grad.astype(jnp.bfloat16)
    up_low = up_grad.astype(jnp.bfloat16)
    gate_turned = jnp.einsum("ld,lf->df", ff_in, gate_low, preferred_element_type=jnp.float32)
    up_turned = jnp.einsum("ld,lf->df", ff_in, up_low, preferred_element_type=jnp.float32)
    ff_in_partial = (
        jnp.einsum("lf,df->ld", gate_low, gate_up_full[0], preferred_element_type=jnp.float32)
        + jnp.einsum("lf,df->ld", up_low, gate_up_full[1], preferred_element_type=jnp.float32)
    ).astype(jnp.bfloat16)
    ff_in_partial, gate_turned_low, up_turned_low = lax.optimization_barrier(
        (
            ff_in_partial,
            gate_turned.astype(jnp.bfloat16),
            up_turned.astype(jnp.bfloat16),
        )
    )
    gate_up_parts = tuple(
        lax.psum_scatter(item, "dp", scatter_dimension=0, tiled=True)
        for item in (gate_turned_low, up_turned_low)
    )
    ff_in_grad = scatter_relative(split_rows(ff_in_partial))
    middle_part, ff_pre_grad = norm_back(middle, gains[2], ff_in_grad)
    middle_grad = top_grad + middle_part
    attn_out_grad, attn_post_grad = norm_back(attn_out, gains[1], middle_grad)
    attn_grad_all = gather_ordered(attn_out_grad.astype(jnp.bfloat16))
    attended_grad = jnp.einsum(
        "ld,de->le", attn_grad_all, output_turned, preferred_element_type=jnp.float32
    ).astype(jnp.bfloat16)
    output_grad_turned = jnp.einsum(
        "ld,le->de", attn_grad_all, attended, preferred_element_type=jnp.float32
    )
    key_grad_all = jnp.zeros(((reach + 1) * length, head_size), jnp.float32)
    value_grad_all = jnp.zeros(((reach + 1) * length, head_size), jnp.float32)
    start = 0
    first_key, query_block, key_block, value_block, scores = block_parts(start)
    probs = jnp.exp(scores - log_totals)
    probs_low = probs.astype(jnp.bfloat16)
    value_grad_all = value_grad_all.at[first_key : first_key + span].add(
        jnp.einsum("qk,qd->kd", probs_low, attended_grad, preferred_element_type=jnp.float32)
    )
    prob_grad = jnp.einsum(
        "qd,kd->qk", attended_grad, value_block, preferred_element_type=jnp.float32
    )
    inner = jnp.sum(probs * prob_grad, axis=-1, keepdims=True)
    score_grad = (probs * (prob_grad - inner)).astype(jnp.bfloat16)
    query_parts = jnp.dot(score_grad, key_block, preferred_element_type=jnp.float32) * score_scale
    key_grad_all = key_grad_all.at[first_key : first_key + span].add(
        jnp.einsum("qk,qd->kd", score_grad, query_block, preferred_element_type=jnp.float32)
        * score_scale
    )
    own_keys = key_grad_all[reach * length :]
    own_values = value_grad_all[reach * length :]
    step = 1
    slot = reach - step
    returned = (
        from_behind(
            key_grad_all[slot * length : (slot + 1) * length].astype(jnp.bfloat16), "dp", -step
        ).astype(jnp.float32),
        from_behind(
            value_grad_all[slot * length : (slot + 1) * length].astype(jnp.bfloat16), "dp", -step
        ).astype(jnp.float32),
    )
    own_keys = own_keys + returned[0]
    own_values = own_values + returned[1]
    unused, query_pull = jax.vjp(
        partial(prepare_head, cosine=cosine, sine=sine), query_pre, gains[4]
    )
    query_pre_grad, query_gain_grad = query_pull(query_parts)
    unused, key_pull = jax.vjp(
        partial(prepare_head, cosine=cosine, sine=sine), key_pre, gains[5]
    )
    key_pre_grad, key_gain_grad = key_pull(own_keys)
    joint_grad_rows = jnp.concatenate([query_pre_grad, key_pre_grad, own_values], axis=1).astype(
        jnp.bfloat16
    )
    joint_grad = jnp.einsum(
        "ld,lc->dc", attn_in, joint_grad_rows, preferred_element_type=jnp.float32
    )
    attn_in_grad = scatter_ordered(
        jnp.einsum(
            "lc,dc->ld", joint_grad_rows, joint_weight, preferred_element_type=jnp.float32
        ).astype(jnp.bfloat16)
    )
    tokens_part, attn_pre_grad = norm_back(residual, gains[0], attn_in_grad)
    tokens_grad = middle_grad + tokens_part
    small_grads = [
        jnp.pad(item.reshape(-1, gain_rows), ((0, 0), (0, rows - gain_rows))).reshape(-1)
        for item in (query_gain_grad, key_gain_grad)
    ]
    gain_grads = jnp.stack(
        [attn_pre_grad, attn_post_grad, ff_pre_grad, ff_post_grad] + small_grads, axis=1
    )
    gain_grads = jnp.pad(gain_grads, ((0, 0), (0, 128 - gain_grads.shape[1])))
    packed_grad = jnp.concatenate(
        [
            joint_grad[:, :head_size].astype(jnp.bfloat16),
            output_grad_turned.astype(jnp.bfloat16),
            joint_grad[:, head_size:].astype(jnp.bfloat16),
            gain_grads.astype(jnp.bfloat16),
        ],
        axis=1,
    )
    down_owned = jnp.transpose(scatter_dp(down_low))
    gate_up_owned = jnp.stack(gate_up_parts, axis=0).astype(jnp.float32)
    packed_owned = scatter_dp(packed_grad)
    query_owned = packed_owned[:, :head_size].astype(jnp.float32)
    output_owned = jnp.transpose(packed_owned[:, head_size : 2 * head_size]).astype(jnp.float32)
    summed = sum_over_mp(packed_owned[:, 2 * head_size :].astype(jnp.bfloat16))
    keyval_owned = summed[:, : 2 * head_size]
    gain_owned = jnp.transpose(summed[:, 2 * head_size :])
    return (
        result,
        tokens_grad,
        query_owned,
        keyval_owned,
        output_owned,
        gate_up_owned,
        down_owned,
        gain_owned[0],
        gain_owned[1],
        gain_owned[2],
        gain_owned[3],
        gain_owned[4, :gain_rows],
        gain_owned[5, :gain_rows],
    )


def solution(mesh):
    placed = (
        P(("dp", "mp"), None),
        P("dp"),
        P("dp"),
        P("dp", "mp"),
        P("dp", None),
        P("mp", "dp"),
        P(None, "dp", "mp"),
        P("mp", "dp"),
        P("dp"),
        P("dp"),
        P("dp"),
        P("dp"),
        P("dp"),
        P("dp"),
        P(("dp", "mp"), None),
    )
    return jax.shard_map(
        local,
        mesh=mesh,
        in_specs=placed,
        out_specs=(
            P(("dp", "mp"), None),
            P(("dp", "mp"), None),
            P("dp", "mp"),
            P("dp", None),
            P("mp", "dp"),
            P(None, "dp", "mp"),
            P("mp", "dp"),
            P("dp"),
            P("dp"),
            P("dp"),
            P("dp"),
            P("dp"),
            P("dp"),
        ),
        check_vma=False,
    )
```
